32 devices in a mesh: grp: 2 (over x), exp: 4 (over y, core), base: 4 (over z).
Axes of the slice: x: 2, y: 2, z: 4, core: 2. Of those that a mesh axis runs over, the one named last changes fastest.
Arguments:
- tokens: bfloat16 [512, 7168], P(('grp', 'exp'), 'base'), parts along dimension 0, may hold values from -6 to 6
- expert_ids: int32 [512, 8], P(('grp', 'exp')), parts along dimension 0, may hold values from 0 to 15, all different within a row; in each aligned block of 64 rows (0 to 63, 64 to 127, ...) at most 48 rows name the same one
- gate_q: int32 [512, 8], P(('grp', 'exp')), parts along dimension 0, may hold values from 1 to 65536
- importance: float32 [7168], P('base'), may hold values from 0.5 to 18
- dense_gate: bfloat16 [16, 7168, 1024], P('exp', None, 'base'), may hold values from -0.0625 to 0.0625
- dense_up: bfloat16 [16, 7168, 1024], P('exp', None, 'base'), may hold values from -0.0625 to 0.0625
- dense_down: bfloat16 [16, 1024, 7168], P('exp', None, 'base'), may hold values from -0.1875 to 0.1875
- delta_gate: bfloat16 [16, 7168, 128], P('exp', None, 'base'), may hold values from -0.0625 to 0.0625
- delta_up: bfloat16 [16, 7168, 128], P('exp', None, 'base'), may hold values from -0.0625 to 0.0625
- delta_down: bfloat16 [16, 128, 7168], P('exp', None, 'base'), may hold values from -0.5 to 0.5
- base_gate: bfloat16 [7168, 1024], P(None, 'base'), may hold values from -0.0625 to 0.0625
- base_up: bfloat16 [7168, 1024], P(None, 'base'), may hold values from -0.0625 to 0.0625
- base_down: bfloat16 [1024, 7168], P('base'), may hold values from -0.1875 to 0.1875
Outputs:
- errors: float32 [512], P(('grp', 'exp')), parts along dimension 0
The draws below stay inside these ranges and needn't reach their ends.
There are 2 independent parts, one for each index of `grp`. The reference program is written for one: setup_inputs(seed, part) draws one part's arguments, and reference() takes and returns one part's arrays. A program takes and returns all parts, laid end to end along the dimension named above; an argument that names none is the same for every part. Nothing has to cross between parts.
Inputs may be any that keep to these rules, and one draw needn't show every extreme that they name: `expert_ids`: A token names 8 different experts; among the tokens of one index of exp no expert is named more than 48 times.
All inputs are finite; a program needn't handle non-finite values.
Results may differ from the reference program's by a relative error of at most 0.00064.
Values may be sent and summed in bfloat16 or wider, within the bound.
A program may use at most 256 MiB of HBM per device.

```python
import math
import jax
import jax.numpy as jnp
import numpy as np
from jax import lax

D = 7168
FF = 1024
SHARED = 1024
RANK = 128
TOP = 8
TOK_EXP = 64
EXPERTS = 16
CAP = 48
TOKENS = 256
N_EXP = 4


def draw_importance(key, part):
    feature = jnp.arange(D, dtype=jnp.float32) / D
    rising = jnp.exp(math.log(3.0) * feature)
    jitter = jnp.exp(jax.random.uniform(key, (D,), jnp.float32, math.log(0.5), math.log(2.0)))
    return (rising * jitter).astype(jnp.float32)


def with_ends(array, rng, smallest, high):
    shape = array.shape
    spot = [jax.random.randint(jax.random.fold_in(rng, axis), (), 0, shape[axis]) for axis in range(len(shape))]
    array = array.at[tuple(spot)].set(smallest)
    longest = shape.index(max(shape))
    spot[longest] = (spot[longest] + 1) % shape[longest]
    return array.at[tuple(spot)].set(high)


def shard_levels(own_key, shape, shards, least, high):
    factor_of, own = 1.0, jax.random.fold_in(own_key, 6)
    for position, blocks in shards:
        draws = jnp.exp(jax.random.uniform(jax.random.fold_in(own, position), (blocks,), jnp.float32, least / len(shards), high / len(shards)))
        factor_of = factor_of * jnp.repeat(draws, shape[position] // blocks).reshape([-1 if axis == position else 1 for axis in range(len(shape))])
    return factor_of


def assign_block(key, own, number, rows, count, top, bound, slope):
    order = jax.random.permutation(key, count)
    crowded, ordinary = shares(count, rows * top, bound, slope, True), shares(count, rows * top, bound, slope, False)
    places = jnp.arange(count)

    def named(tallies, rotation):
        used = int((tallies > 0).sum())
        fixed = max(1, used // 4)
        moved = fixed + (places - fixed + rotation * (used - fixed)) % max(1, count - fixed)
        return jnp.zeros((count,), jnp.int32).at[order[jnp.where(places < fixed, places, moved)]].set(jnp.asarray(tallies, jnp.int32))

    tallies = jnp.where(number % 4 == 0, named(crowded, number // 4), named(ordinary, number - number // 4 - 1))
    mixed = jax.random.permutation(jax.random.fold_in(own, 3), count)
    giver, sink = mixed[0:count // 2 * 2:2], mixed[1:count // 2 * 2:2]
    room = jnp.minimum(tallies[giver] - 1, bound - tallies[sink]) // 2
    room = jnp.where((giver == order[0]) | (sink == order[0]) | (tallies[sink] == 0), 0, jnp.maximum(room, 0))
    moved = jax.random.randint(jax.random.fold_in(own, 4), (count // 2,), 0, 1 << 20) % (room + 1)
    tallies = tallies.at[giver].add(-moved).at[sink].add(moved)
    items = jnp.searchsorted(jnp.cumsum(tallies), jnp.arange(rows * top), side="right").astype(jnp.int32)
    table = items.reshape(top, rows).T
    table = table[jax.random.permutation(jax.random.fold_in(own, 1), rows)]
    rotation = jax.random.randint(jax.random.fold_in(own, 2), (rows, 1), 0, top)
    return jnp.take_along_axis(table, (jnp.arange(top)[None, :] + rotation) % top, axis=1)


def shares(count, total, most, skew, full):
    loads = [(1 << 20) // math.isqrt(grade ** skew) + 1 for grade in range(1, count + 1)]
    largest = most if full else min(most, max(-(-total // count), total * loads[0] // sum(loads)))
    least = 1 if total - largest >= count - 1 else 0
    given, rest = [largest] + [least] * (count - 1), total - largest - least * (count - 1)
    while rest > 0:
        free = [i for i in range(1, count) if given[i] < largest] or [i for i in range(1, count) if given[i] < most]
        whole, budget = sum([loads[i] for i in free]), rest
        for i in free:
            more = min(most - given[i], max(1, budget * loads[i] // whole), rest)
            given[i] = given[i] + more
            rest = rest - more
    return np.array(given)


def centred(stream_key, shape, width, limit, pieces=(), kind=jnp.bfloat16):
    result = width * jax.random.normal(stream_key, shape, jnp.float32)
    if pieces:
        result = result * shard_levels(stream_key, shape, pieces, -0.22, 0.18)
    return jnp.clip(result, -limit, limit).astype(kind)


def setup_inputs(seed: int = 0, part: int = 0) -> dict:
    key_list = jax.random.split(jax.random.key(seed), 14)
    own_keys = jax.random.split(jax.random.fold_in(key_list[13], part), 14)
    tokens = centred(own_keys[0], (TOKENS, D), 1.0, 6.0, ((0, 4), (1, 4)))
    expert_ids_keys = jax.random.split(jax.random.fold_in(own_keys[1], 1), TOKENS // TOK_EXP)
    expert_ids_turns = jax.random.permutation(jax.random.fold_in(own_keys[1], 3), TOKENS // TOK_EXP)
    expert_ids = jax.vmap(lambda own, number: assign_block(jax.random.fold_in(own_keys[1], 2), own, number, TOK_EXP, EXPERTS, TOP, CAP, 2))(expert_ids_keys, expert_ids_turns).reshape((TOKENS, TOP))
    gate_q = with_ends(jax.random.randint(own_keys[2], (TOKENS, TOP), 1, 65537), jax.random.fold_in(own_keys[2], 1), 1, 65536).astype(jnp.int32)
    importance = draw_importance(jax.random.fold_in(key_list[13], 71), part)
    dense_gate = centred(key_list[4], (EXPERTS, D, FF), D ** -0.5, 0.0625, ((0, 4), (2, 4)))
    dense_up = centred(key_list[5], (EXPERTS, D, FF), D ** -0.5, 0.0625, ((0, 4), (2, 4)))
    dense_down = centred(key_list[6], (EXPERTS, FF, D), FF ** -0.5, 0.1875, ((0, 4), (2, 4)))
    delta_gate = centred(key_list[7], (EXPERTS, D, RANK), D ** -0.5, 0.0625, ((0, 4), (2, 4)))
    delta_up = centred(key_list[8], (EXPERTS, D, RANK), D ** -0.5, 0.0625, ((0, 4), (2, 4)))
    delta_down = centred(key_list[9], (EXPERTS, RANK, D), RANK ** -0.5, 0.5, ((0, 4), (2, 4)))
    base_gate = centred(key_list[10], (D, SHARED), D ** -0.5, 0.0625, ((1, 4),))
    base_up = centred(key_list[11], (D, SHARED), D ** -0.5, 0.0625, ((1, 4),))
    base_down = centred(key_list[12], (SHARED, D), SHARED ** -0.5, 0.1875, ((0, 4),))
    return dict(tokens=tokens, expert_ids=expert_ids, gate_q=gate_q, importance=importance, dense_gate=dense_gate, dense_up=dense_up, dense_down=dense_down, delta_gate=delta_gate, delta_up=delta_up, delta_down=delta_down, base_gate=base_gate, base_up=base_up, base_down=base_down)


def slot_positions(expert_ids):
    blocks = expert_ids.reshape(N_EXP, TOK_EXP * TOP)
    onehot = (blocks[:, :, None] == jnp.arange(EXPERTS, dtype=jnp.int32)[None, None, :]).astype(jnp.int32)
    before = jnp.cumsum(onehot, axis=1) - onehot
    return jnp.sum(before * onehot, axis=2).reshape(TOKENS, TOP).astype(jnp.int32)


def swiglu(gathered, gate_w, up_w):
    gate_pre = jnp.dot(gathered, gate_w, preferred_element_type=jnp.float32)
    upper = jnp.dot(gathered, up_w, preferred_element_type=jnp.float32)
    return (jax.nn.silu(gate_pre) * upper).astype(jnp.bfloat16)


def reference(tokens, expert_ids, gate_q, importance, dense_gate, dense_up, dense_down, delta_gate, delta_up, delta_down, base_gate, base_up, base_down):
    positions = slot_positions(expert_ids)
    source = (jnp.arange(TOKENS, dtype=jnp.int32) // TOK_EXP)[:, None]
    slots = (source * CAP + positions).astype(jnp.int32)
    owners = jnp.broadcast_to(jnp.arange(TOKENS, dtype=jnp.int32)[:, None], (TOKENS, TOP))
    slot_table = jnp.full((EXPERTS, N_EXP * CAP), TOKENS, jnp.int32).at[expert_ids, slots].set(owners)
    padded = jnp.concatenate([tokens, jnp.zeros((1, D), tokens.dtype)], axis=0)

    def one_expert(items):
        row_index, gate_dense, up_dense, down_dense, gate_low, up_low, down_low = items
        gathered = padded[row_index]
        hidden = swiglu(gathered, gate_dense, up_dense)
        low_rank = swiglu(gathered, gate_low, up_low)
        output = jnp.dot(hidden, down_dense, preferred_element_type=jnp.float32) - jnp.dot(low_rank, down_low, preferred_element_type=jnp.float32)
        return output.astype(jnp.bfloat16)

    residual = lax.map(one_expert, (slot_table, dense_gate, dense_up, dense_down, delta_gate, delta_up, delta_down))
    residual = lax.optimization_barrier(residual)
    shared = swiglu(tokens, base_gate, base_up)
    base_out = jnp.dot(shared, base_down, preferred_element_type=jnp.float32).astype(jnp.bfloat16)
    base_out = lax.optimization_barrier(base_out)
    picked = residual[expert_ids, slots].astype(jnp.float32)
    deviation = picked - base_out.astype(jnp.float32)[:, None, :]
    squares = jnp.sum(importance * deviation * deviation, axis=2)
    weights = gate_q.astype(jnp.float32) / 65536.0
    return jnp.sum(weights * squares, axis=1) / D
```

```python
import jax
import jax.numpy as jnp
from jax import lax
from jax.sharding import PartitionSpec as P

D = 7168


def swiglu(rows, gate_w, up_w):
    gate_pre = jnp.dot(rows, gate_w, preferred_element_type=jnp.float32)
    up_pre = jnp.dot(rows, up_w, preferred_element_type=jnp.float32)
    return (jax.nn.silu(gate_pre) * up_pre).astype(jnp.bfloat16)


def shards(
    tokens,
    expert_ids,
    gate_q,
    importance,
    dense_gate,
    dense_up,
    dense_down,
    delta_gate,
    delta_up,
    delta_down,
    base_gate,
    base_up,
    base_down,
):
    groups = lax.axis_size("exp")
    splits = lax.axis_size("base")
    tok_rows, local_width = tokens.shape
    top_k = expert_ids.shape[1]
    local_experts = dense_gate.shape[0]
    capacity = tok_rows * top_k * 3 // (2 * local_experts * groups)
    dense_width = dense_gate.shape[2]
    low_width = delta_gate.shape[2]
    all_rows = tok_rows * groups
    slots = capacity * groups

    routing = lax.all_gather(
        jnp.concatenate([expert_ids, gate_q], axis=1), "exp", axis=0, tiled=True
    )
    own_rows = lax.all_gather(tokens, "base", axis=1, tiled=True)
    rows = lax.all_gather(own_rows, "exp", axis=0, tiled=True)

    ids, gates = routing[:, :top_k], routing[:, top_k:]
    first = lax.axis_index("exp") * local_experts
    mine = first + jnp.arange(local_experts, dtype=jnp.int32)
    hit = ids[:, None, :] == mine[None, :, None]
    weight = jnp.sum(jnp.where(hit, gates[:, None, :].astype(jnp.float32), 0.0), axis=2) / 65536.0
    named = jnp.any(hit, axis=2)
    order = jnp.arange(all_rows, dtype=jnp.int32)
    block = order // tok_rows
    before = (block[:, None] == block[None, :]) & (order[None, :] < order[:, None])
    position = jnp.dot(
        before.astype(jnp.bfloat16), named.astype(jnp.bfloat16), preferred_element_type=jnp.float32
    ).astype(jnp.int32)
    slot = jnp.where(named, block[:, None] * capacity + position, -1)
    pick = jnp.arange(slots, dtype=jnp.int32)[None, :, None] == slot.T[:, None, :]
    select = pick.astype(jnp.bfloat16)

    shared = swiglu(own_rows, base_gate, base_up)
    partial_value = jnp.dot(shared, base_down, preferred_element_type=jnp.float32)
    base_own = lax.psum_scatter(
        partial_value.astype(jnp.bfloat16), "base", scatter_dimension=1, tiled=True
    )
    base_all = lax.all_gather(base_own, "exp", axis=0, tiled=True)

    packed = []
    for j in range(local_experts):
        hidden = swiglu(rows, dense_gate[j], dense_up[j])
        low = swiglu(rows, delta_gate[j], delta_up[j])
        both = jnp.concatenate([hidden, low], axis=1)
        packed.append(
            jnp.dot(select[j], both, preferred_element_type=jnp.float32).astype(jnp.bfloat16)
        )
    sent = jnp.stack(packed)
    full = lax.all_gather(sent, "base", axis=0, tiled=False)

    total = jnp.zeros((all_rows,), jnp.float32)
    for j in range(local_experts):
        hid = jnp.concatenate([full[b, j, :, :dense_width] for b in range(splits)], axis=1)
        low = jnp.concatenate([full[b, j, :, dense_width:] for b in range(splits)], axis=1)
        residual = jnp.dot(hid, dense_down[j], preferred_element_type=jnp.float32) - jnp.dot(
            low, delta_down[j], preferred_element_type=jnp.float32
        )
        residual = residual.astype(jnp.bfloat16).astype(jnp.float32)
        base_rows = jnp.dot(select[j], base_all, preferred_element_type=jnp.float32)
        deviation = residual - base_rows
        squares = jnp.sum(importance * deviation * deviation, axis=1)
        back = jnp.sum(jnp.where(pick[j], squares[:, None], 0.0), axis=0)
        total = total + weight[:, j] * back
    total = lax.psum(total / D, ("exp", "base"))
    return lax.dynamic_slice_in_dim(total, lax.axis_index("exp") * tok_rows, tok_rows)


def solution(mesh):
    in_specs = (
        P(("grp", "exp"), "base"),
        P(("grp", "exp"), None),
        P(("grp", "exp"), None),
        P("base"),
        P("exp", None, "base"),
        P("exp", None, "base"),
        P("exp", None, "base"),
        P("exp", None, "base"),
        P("exp", None, "base"),
        P("exp", None, "base"),
        P(None, "base"),
        P(None, "base"),
        P("base", None),
    )
    out_specs = P(("grp", "exp"))
    return jax.shard_map(shards, mesh=mesh, in_specs=in_specs, out_specs=out_specs, check_vma=False)
```

```python
import functools

import jax
import jax.numpy as jnp
from jax import lax
from jax.experimental import pallas as pl
from jax.experimental.pallas import tpu as pltpu
from jax.sharding import PartitionSpec as P

D = 7168


def sum_kernel(groups, splits, part_ref, out_ref, held, send_sem, recv_sem):
    n = groups * splits
    mine = lax.axis_index("exp")
    me = mine * splits + lax.axis_index("base")

    def where(off):
        peer = lax.rem(me + off, n)
        return peer, {"exp": peer // splits, "base": lax.rem(peer, splits)}

    barrier = pltpu.get_barrier_semaphore()

    @pl.loop(1, n)
    def _(off):
        pl.semaphore_signal(
            barrier, inc=1, device_id=where(off)[1], device_id_type=pl.DeviceIdType.MESH
        )

    pl.semaphore_wait(barrier, n - 1)

    def copy(block, slot, off, device):
        return pltpu.make_async_remote_copy(
            src_ref=part_ref.at[block],
            dst_ref=held.at[slot],
            send_sem=send_sem.at[off],
            recv_sem=recv_sem.at[slot],
            device_id=device,
            device_id_type=pl.DeviceIdType.MESH,
        )

    @pl.loop(1, n)
    def _(off):
        device = where(off)[1]
        copy(device["exp"], me, off, device).start()

    held[me] = part_ref[mine]

    @pl.loop(1, n)
    def _(off):
        peer, device = where(off)
        arrived = copy(mine, peer, off, device)
        arrived.wait_recv()
        arrived.wait_send()

    total = held[0]
    for source in range(1, n):
        total = total + held[source]
    out_ref[...] = total


def sum_over_group(total, groups, splits):
    tok_rows = total.shape[0] // groups
    lanes = -(-tok_rows // 128) * 128
    n = groups * splits
    part = jnp.pad(total.reshape(groups, 1, tok_rows), ((0, 0), (0, 7), (0, lanes - tok_rows)))
    out = pl.pallas_call(
        functools.partial(sum_kernel, groups, splits),
        out_shape=jax.ShapeDtypeStruct((8, lanes), jnp.float32),
        in_specs=[pl.BlockSpec(memory_space=pltpu.VMEM)],
        out_specs=pl.BlockSpec(memory_space=pltpu.VMEM),
        scratch_shapes=[
            pltpu.VMEM((n, 8, lanes), jnp.float32),
            pltpu.SemaphoreType.DMA((n,)),
            pltpu.SemaphoreType.DMA((n,)),
        ],
        compiler_params=pltpu.CompilerParams(collective_id=0, has_side_effects=True),
    )(part)
    return out[0, :tok_rows]


def swiglu(rows, gate_w, up_w):
    gate_pre = jnp.dot(rows, gate_w, preferred_element_type=jnp.float32)
    up_pre = jnp.dot(rows, up_w, preferred_element_type=jnp.float32)
    return (jax.nn.silu(gate_pre) * up_pre).astype(jnp.bfloat16)


def shards(
    tokens,
    expert_ids,
    gate_q,
    importance,
    dense_gate,
    dense_up,
    dense_down,
    delta_gate,
    delta_up,
    delta_down,
    base_gate,
    base_up,
    base_down,
):
    groups = lax.axis_size("exp")
    splits = lax.axis_size("base")
    tok_rows, local_width = tokens.shape
    top_k = expert_ids.shape[1]
    local_experts = dense_gate.shape[0]
    capacity = tok_rows * top_k * 3 // (2 * local_experts * groups)
    dense_width = dense_gate.shape[2]
    low_width = delta_gate.shape[2]
    all_rows = tok_rows * groups
    slots = capacity * groups

    routing = lax.all_gather(
        jnp.concatenate([expert_ids, gate_q], axis=1), "exp", axis=0, tiled=True
    )
    own_rows = lax.all_gather(tokens, "base", axis=1, tiled=True)
    rows = lax.all_gather(own_rows, "exp", axis=0, tiled=True)

    ids, gates = routing[:, :top_k], routing[:, top_k:]
    first = lax.axis_index("exp") * local_experts
    mine = first + jnp.arange(local_experts, dtype=jnp.int32)
    hit = ids[:, None, :] == mine[None, :, None]
    weight = jnp.sum(jnp.where(hit, gates[:, None, :].astype(jnp.float32), 0.0), axis=2) / 65536.0
    named = jnp.any(hit, axis=2)
    order = jnp.arange(all_rows, dtype=jnp.int32)
    block = order // tok_rows
    before = (block[:, None] == block[None, :]) & (order[None, :] < order[:, None])
    position = jnp.dot(
        before.astype(jnp.bfloat16), named.astype(jnp.bfloat16), preferred_element_type=jnp.float32
    ).astype(jnp.int32)
    slot = jnp.where(named, block[:, None] * capacity + position, -1)
    pick = jnp.arange(slots, dtype=jnp.int32)[None, :, None] == slot.T[:, None, :]
    select = pick.astype(jnp.bfloat16)

    shared = swiglu(own_rows, base_gate, base_up)
    partial_value = jnp.dot(shared, base_down, preferred_element_type=jnp.float32)
    base_own = lax.psum_scatter(
        partial_value.astype(jnp.bfloat16), "base", scatter_dimension=1, tiled=True
    )
    base_all = lax.all_gather(base_own, "exp", axis=0, tiled=True)

    contract = (((1,), (1,)), ((), ()))
    low_gates = delta_gate.transpose(0, 2, 1).reshape(local_experts * low_width, -1)
    low_ups = delta_up.transpose(0, 2, 1).reshape(local_experts * low_width, -1)
    low_pre = lax.dot_general(rows, low_gates, contract, preferred_element_type=jnp.float32)
    low_up = lax.dot_general(rows, low_ups, contract, preferred_element_type=jnp.float32)
    low_all = (jax.nn.silu(low_pre) * low_up).astype(jnp.bfloat16)

    packed = []
    for j in range(local_experts):
        hidden = swiglu(rows, dense_gate[j], dense_up[j])
        low = low_all[:, j * low_width : (j + 1) * low_width]
        both = jnp.concatenate([hidden, low], axis=1)
        packed.append(
            jnp.dot(select[j], both, preferred_element_type=jnp.float32).astype(jnp.bfloat16)
        )
    sent = jnp.stack(packed)
    full = lax.all_gather(sent, "base", axis=0, tiled=False)

    total = jnp.zeros((all_rows,), jnp.float32)
    for j in range(local_experts):
        hid = jnp.concatenate([full[b, j, :, :dense_width] for b in range(splits)], axis=1)
        low = jnp.concatenate([full[b, j, :, dense_width:] for b in range(splits)], axis=1)
        residual = jnp.dot(hid, dense_down[j], preferred_element_type=jnp.float32) - jnp.dot(
            low, delta_down[j], preferred_element_type=jnp.float32
        )
        residual = residual.astype(jnp.bfloat16).astype(jnp.float32)
        base_rows = jnp.dot(select[j], base_all, preferred_element_type=jnp.float32)
        deviation = residual - base_rows
        squares = jnp.sum(importance * deviation * deviation, axis=1)
        back = jnp.sum(jnp.where(pick[j], squares[:, None], 0.0), axis=0)
        total = total + weight[:, j] * back
    return sum_over_group(total / D, groups, splits)


def solution(mesh):
    in_specs = (
        P(("grp", "exp"), "base"),
        P(("grp", "exp"), None),
        P(("grp", "exp"), None),
        P("base"),
        P("exp", None, "base"),
        P("exp", None, "base"),
        P("exp", None, "base"),
        P("exp", None, "base"),
        P("exp", None, "base"),
        P("exp", None, "base"),
        P(None, "base"),
        P(None, "base"),
        P("base", None),
    )
    out_specs = P(("grp", "exp"))
    return jax.shard_map(shards, mesh=mesh, in_specs=in_specs, out_specs=out_specs, check_vma=False)
```

```python
import functools

import jax
import jax.numpy as jnp
from jax import lax
from jax.experimental import pallas as pl
from jax.experimental.pallas import tpu as pltpu
from jax.sharding import PartitionSpec as P

D = 7168


def sum_kernel(groups, splits, part_ref, out_ref, held, send_sem, recv_sem):
    n = groups * splits
    mine = lax.axis_index("exp")
    me = mine * splits + lax.axis_index("base")

    def where(off):
        peer = lax.rem(me + off, n)
        return peer, {"exp": peer // splits, "base": lax.rem(peer, splits)}

    barrier = pltpu.get_barrier_semaphore()

    @pl.loop(1, n)
    def _(off):
        pl.semaphore_signal(
            barrier, inc=1, device_id=where(off)[1], device_id_type=pl.DeviceIdType.MESH
        )

    pl.semaphore_wait(barrier, n - 1)

    def copy(block, slot, off, device):
        return pltpu.make_async_remote_copy(
            src_ref=part_ref.at[block],
            dst_ref=held.at[slot],
            send_sem=send_sem.at[off],
            recv_sem=recv_sem.at[slot],
            device_id=device,
            device_id_type=pl.DeviceIdType.MESH,
        )

    @pl.loop(1, n)
    def _(off):
        device = where(off)[1]
        copy(device["exp"], me, off, device).start()

    held[me] = part_ref[mine]

    @pl.loop(1, n)
    def _(off):
        peer, device = where(off)
        arrived = copy(mine, peer, off, device)
        arrived.wait_recv()
        arrived.wait_send()

    total = held[0]
    for source in range(1, n):
        total = total + held[source]
    out_ref[...] = total


def sum_over_group(total, groups, splits):
    tok_rows = total.shape[0] // groups
    lanes = -(-tok_rows // 128) * 128
    n = groups * splits
    part = jnp.pad(total.reshape(groups, 1, tok_rows), ((0, 0), (0, 7), (0, lanes - tok_rows)))
    out = pl.pallas_call(
        functools.partial(sum_kernel, groups, splits),
        out_shape=jax.ShapeDtypeStruct((8, lanes), jnp.float32),
        in_specs=[pl.BlockSpec(memory_space=pltpu.VMEM)],
        out_specs=pl.BlockSpec(memory_space=pltpu.VMEM),
        scratch_shapes=[
            pltpu.VMEM((n, 8, lanes), jnp.float32),
            pltpu.SemaphoreType.DMA((n,)),
            pltpu.SemaphoreType.DMA((n,)),
        ],
        compiler_params=pltpu.CompilerParams(collective_id=0, has_side_effects=True),
    )(part)
    return out[0, :tok_rows]


def tile_of(width, sizes):
    return next((size for size in sizes if width % size == 0), width)


def expert_kernel(
    splits,
    rows_ref,
    select_ref,
    low_ref,
    gate_ref,
    up_ref,
    down_ref,
    low_down_ref,
    out_ref,
    gate_buf,
    up_buf,
    down_buf,
    hidden,
    lows,
    gate_acc,
    up_acc,
    load_sem,
    down_sem,
    send_sem,
    recv_sem,
):
    experts, depth, width = gate_ref.shape
    local_width = down_ref.shape[2]
    low_width = low_ref.shape[1] // experts
    last = splits - 1
    me = lax.axis_index("base")
    barrier = pltpu.get_barrier_semaphore()

    def load(j):
        slot = j % 2
        return (
            pltpu.make_async_copy(gate_ref.at[j], gate_buf.at[slot], load_sem.at[0, slot]),
            pltpu.make_async_copy(up_ref.at[j], up_buf.at[slot], load_sem.at[1, slot]),
        )

    def load_down(j):
        return pltpu.make_async_copy(down_ref.at[j], down_buf.at[j], down_sem.at[j])

    for j in range(min(2, experts)):
        for copy in load(j):
            copy.start()

    for off in range(1, splits):
        pl.semaphore_signal(
            barrier,
            inc=1,
            device_id={"base": lax.rem(me + off, splits)},
            device_id_type=pl.DeviceIdType.MESH,
        )
    pl.semaphore_wait(barrier, last)

    def passing(item, source, way):
        step = 1 if way == 0 else -1
        ref = lows.at[source] if item == experts else hidden.at[source, item]
        return pltpu.make_async_remote_copy(
            src_ref=ref,
            dst_ref=ref,
            send_sem=send_sem.at[way, source, item],
            recv_sem=recv_sem.at[source, item],
            device_id={"base": me + step},
            device_id_type=pl.DeviceIdType.MESH,
        )

    def relay(item, far):
        if far == 0:
            for way, inside in ((0, me < last), (1, me > 0)):

                @pl.when(inside)
                def _(way=way):
                    passing(item, me, way).start()

            return
        for way, source, inside, on in (
            (0, me - far, me >= far, me < last),
            (1, me + far, me + far <= last, me > 0),
        ):

            @pl.when(inside)
            def _(way=way, source=source):
                passing(item, source, way).wait_recv()

            @pl.when(jnp.logical_and(inside, on))
            def _(way=way, source=source):
                passing(item, source, way).start()

    lows[me] = low_ref[...]
    relay(experts, 0)

    chunk = tile_of(depth, (1024, 512, 256, 128))
    tile = tile_of(local_width, (256, 128))

    def first_half(j):
        for copy in load(j):
            copy.wait()
        slot = j % 2
        gate_acc[...] = jnp.zeros_like(gate_acc)
        up_acc[...] = jnp.zeros_like(up_acc)

        @pl.loop(0, depth // chunk)
        def _(c):
            part = pl.ds(pl.multiple_of(c * chunk, chunk), chunk)
            block = rows_ref[:, part]
            gate_acc[...] += jnp.dot(
                block, gate_buf[slot, part, :], preferred_element_type=jnp.float32
            )
            up_acc[...] += jnp.dot(block, up_buf[slot, part, :], preferred_element_type=jnp.float32)

        if j + 2 < experts:
            for copy in load(j + 2):
                copy.start()
        load_down(j).start()
        value = gate_acc[...]
        both = (value / (1.0 + jnp.exp(-value)) * up_acc[...]).astype(jnp.bfloat16)
        hidden[me, j] = jnp.dot(
            select_ref[j], both, preferred_element_type=jnp.float32
        ).astype(jnp.bfloat16)

    def second_half(j):
        load_down(j).wait()
        picked = []
        for b in range(splits):
            chosen = jnp.dot(select_ref[j], lows[b], preferred_element_type=jnp.float32)
            picked.append(chosen[:, j * low_width : (j + 1) * low_width].astype(jnp.bfloat16))

        @pl.loop(0, local_width // tile)
        def _(c):
            part = pl.ds(pl.multiple_of(c * tile, tile), tile)
            total = jnp.zeros((out_ref.shape[1], tile), jnp.float32)
            for b in range(splits):
                total += jnp.dot(
                    hidden[b, j],
                    down_buf[j, b * width : (b + 1) * width, part],
                    preferred_element_type=jnp.float32,
                )
            for b in range(splits):
                total -= jnp.dot(
                    picked[b],
                    low_down_ref[j, b * low_width : (b + 1) * low_width, part],
                    preferred_element_type=jnp.float32,
                )
            out_ref[j, :, part] = total.astype(jnp.bfloat16)

    for step in range(experts + last):
        if step < experts:
            first_half(step)
            relay(step, 0)
        for far in range(1, splits):
            if far == step + 1:
                relay(experts, far)
            if 0 <= step - far < experts:
                relay(step - far, far)
        if step >= last:
            second_half(step - last)

    for item in range(experts + 1):
        for source in range(splits):
            for way, inside in (
                (0, jnp.logical_and(me >= source, me < last)),
                (1, jnp.logical_and(me <= source, me > 0)),
            ):

                @pl.when(inside)
                def _(item=item, source=source, way=way):
                    passing(item, source, way).wait_send()


def run_experts(rows, select, low_all, gate, up, down, low_down, splits):
    experts, depth, width = gate.shape
    slots = select.shape[1]
    all_rows = rows.shape[0]
    local_width = down.shape[2]
    vmem, hbm = pl.BlockSpec(memory_space=pltpu.VMEM), pl.BlockSpec(memory_space=pl.ANY)
    flops = 2 * experts * (2 * all_rows * depth * width + slots * splits * width * local_width)
    moved = 2 * experts * (2 * depth * width + splits * width * local_width)
    return pl.pallas_call(
        functools.partial(expert_kernel, splits),
        out_shape=jax.ShapeDtypeStruct((experts, slots, local_width), jnp.bfloat16),
        in_specs=[vmem, vmem, vmem, hbm, hbm, hbm, vmem],
        out_specs=vmem,
        scratch_shapes=[
            pltpu.VMEM((2, depth, width), jnp.bfloat16),
            pltpu.VMEM((2, depth, width), jnp.bfloat16),
            pltpu.VMEM(down.shape, jnp.bfloat16),
            pltpu.VMEM((splits, experts, slots, width), jnp.bfloat16),
            pltpu.VMEM((splits,) + low_all.shape, jnp.bfloat16),
            pltpu.VMEM((all_rows, width), jnp.float32),
            pltpu.VMEM((all_rows, width), jnp.float32),
            pltpu.SemaphoreType.DMA((2, 2)),
            pltpu.SemaphoreType.DMA((experts,)),
            pltpu.SemaphoreType.DMA((2, splits, experts + 1)),
            pltpu.SemaphoreType.DMA((splits, experts + 1)),
        ],
        compiler_params=pltpu.CompilerParams(
            collective_id=1, has_side_effects=True, vmem_limit_bytes=54 * 1024 * 1024
        ),
        cost_estimate=pl.CostEstimate(flops=flops, bytes_accessed=moved, transcendentals=0),
    )(rows, select, low_all, gate, up, down, low_down)


def swiglu(rows, gate_w, up_w):
    gate_pre = jnp.dot(rows, gate_w, preferred_element_type=jnp.float32)
    up_pre = jnp.dot(rows, up_w, preferred_element_type=jnp.float32)
    return (jax.nn.silu(gate_pre) * up_pre).astype(jnp.bfloat16)


def shards(
    tokens,
    expert_ids,
    gate_q,
    importance,
    dense_gate,
    dense_up,
    dense_down,
    delta_gate,
    delta_up,
    delta_down,
    base_gate,
    base_up,
    base_down,
):
    groups = lax.axis_size("exp")
    splits = lax.axis_size("base")
    tok_rows, local_width = tokens.shape
    top_k = expert_ids.shape[1]
    local_experts = dense_gate.shape[0]
    capacity = tok_rows * top_k * 3 // (2 * local_experts * groups)
    low_width = delta_gate.shape[2]
    all_rows = tok_rows * groups
    slots = capacity * groups

    routing = lax.all_gather(
        jnp.concatenate([expert_ids, gate_q], axis=1), "exp", axis=0, tiled=True
    )
    own_rows = lax.all_gather(tokens, "base", axis=1, tiled=True)
    rows = lax.all_gather(own_rows, "exp", axis=0, tiled=True)

    ids, gates = routing[:, :top_k], routing[:, top_k:]
    first = lax.axis_index("exp") * local_experts
    mine = first + jnp.arange(local_experts, dtype=jnp.int32)
    hit = ids[:, None, :] == mine[None, :, None]
    weight = jnp.sum(jnp.where(hit, gates[:, None, :].astype(jnp.float32), 0.0), axis=2) / 65536.0
    named = jnp.any(hit, axis=2)
    order = jnp.arange(all_rows, dtype=jnp.int32)
    block = order // tok_rows
    before = (block[:, None] == block[None, :]) & (order[None, :] < order[:, None])
    position = jnp.dot(
        before.astype(jnp.bfloat16), named.astype(jnp.bfloat16), preferred_element_type=jnp.float32
    ).astype(jnp.int32)
    slot = jnp.where(named, block[:, None] * capacity + position, -1)
    pick = jnp.arange(slots, dtype=jnp.int32)[None, :, None] == slot.T[:, None, :]
    select = pick.astype(jnp.bfloat16)

    shared = swiglu(own_rows, base_gate, base_up)
    partial_value = jnp.dot(shared, base_down, preferred_element_type=jnp.float32)
    base_own = lax.psum_scatter(
        partial_value.astype(jnp.bfloat16), "base", scatter_dimension=1, tiled=True
    )
    base_all = lax.all_gather(base_own, "exp", axis=0, tiled=True)

    contract = (((1,), (1,)), ((), ()))
    low_gates = delta_gate.transpose(0, 2, 1).reshape(local_experts * low_width, -1)
    low_ups = delta_up.transpose(0, 2, 1).reshape(local_experts * low_width, -1)
    low_pre = lax.dot_general(rows, low_gates, contract, preferred_element_type=jnp.float32)
    low_up = lax.dot_general(rows, low_ups, contract, preferred_element_type=jnp.float32)
    low_all = (jax.nn.silu(low_pre) * low_up).astype(jnp.bfloat16)

    residuals = run_experts(
        rows, select, low_all, dense_gate, dense_up, dense_down, delta_down, splits
    )

    total = jnp.zeros((all_rows,), jnp.float32)
    for j in range(local_experts):
        residual = residuals[j].astype(jnp.float32)
        base_rows = jnp.dot(select[j], base_all, preferred_element_type=jnp.float32)
        deviation = residual - base_rows
        squares = jnp.sum(importance * deviation * deviation, axis=1)
        back = jnp.sum(jnp.where(pick[j], squares[:, None], 0.0), axis=0)
        total = total + weight[:, j] * back
    return sum_over_group(total / D, groups, splits)


def solution(mesh):
    in_specs = (
        P(("grp", "exp"), "base"),
        P(("grp", "exp"), None),
        P(("grp", "exp"), None),
        P("base"),
        P("exp", None, "base"),
        P("exp", None, "base"),
        P("exp", None, "base"),
        P("exp", None, "base"),
        P("exp", None, "base"),
        P("exp", None, "base"),
        P(None, "base"),
        P(None, "base"),
        P("base", None),
    )
    out_specs = P(("grp", "exp"))
    return jax.shard_map(shards, mesh=mesh, in_specs=in_specs, out_specs=out_specs, check_vma=False)
```

```python
import functools

import jax
import jax.numpy as jnp
from jax import lax
from jax.experimental import pallas as pl
from jax.experimental.pallas import tpu as pltpu
from jax.sharding import PartitionSpec as P

D = 7168


def sum_kernel(groups, splits, part_ref, out_ref, held, send_sem, recv_sem):
    n = groups * splits
    mine = lax.axis_index("exp")
    me = mine * splits + lax.axis_index("base")

    def where(off):
        peer = lax.rem(me + off, n)
        return peer, {"exp": peer // splits, "base": lax.rem(peer, splits)}

    barrier = pltpu.get_barrier_semaphore()

    @pl.loop(1, n)
    def _(off):
        pl.semaphore_signal(
            barrier, inc=1, device_id=where(off)[1], device_id_type=pl.DeviceIdType.MESH
        )

    pl.semaphore_wait(barrier, n - 1)

    def copy(block, slot, off, device):
        return pltpu.make_async_remote_copy(
            src_ref=part_ref.at[block],
            dst_ref=held.at[slot],
            send_sem=send_sem.at[off],
            recv_sem=recv_sem.at[slot],
            device_id=device,
            device_id_type=pl.DeviceIdType.MESH,
        )

    @pl.loop(1, n)
    def _(off):
        device = where(off)[1]
        copy(device["exp"], me, off, device).start()

    held[me] = part_ref[mine]

    @pl.loop(1, n)
    def _(off):
        peer, device = where(off)
        arrived = copy(mine, peer, off, device)
        arrived.wait_recv()
        arrived.wait_send()

    total = held[0]
    for source in range(1, n):
        total = total + held[source]
    out_ref[...] = total


def sum_over_group(total, groups, splits):
    tok_rows = total.shape[0] // groups
    lanes = -(-tok_rows // 128) * 128
    n = groups * splits
    part = jnp.pad(total.reshape(groups, 1, tok_rows), ((0, 0), (0, 7), (0, lanes - tok_rows)))
    out = pl.pallas_call(
        functools.partial(sum_kernel, groups, splits),
        out_shape=jax.ShapeDtypeStruct((8, lanes), jnp.float32),
        in_specs=[pl.BlockSpec(memory_space=pltpu.VMEM)],
        out_specs=pl.BlockSpec(memory_space=pltpu.VMEM),
        scratch_shapes=[
            pltpu.VMEM((n, 8, lanes), jnp.float32),
            pltpu.SemaphoreType.DMA((n,)),
            pltpu.SemaphoreType.DMA((n,)),
        ],
        compiler_params=pltpu.CompilerParams(collective_id=0, has_side_effects=True),
    )(part)
    return out[0, :tok_rows]


def tile_of(width, sizes):
    return next((size for size in sizes if width % size == 0), width)


def expert_kernel(
    splits,
    groups,
    rows_ref,
    select_ref,
    low_ref,
    gate_ref,
    up_ref,
    down_ref,
    low_down_ref,
    base_ref,
    out_ref,
    bases,
    gate_buf,
    up_buf,
    down_buf,
    hidden,
    lows,
    gate_acc,
    up_acc,
    load_sem,
    down_sem,
    send_sem,
    recv_sem,
    base_send,
    base_recv,
):
    experts, depth, width = gate_ref.shape
    local_width = down_ref.shape[2]
    low_width = low_ref.shape[1] // experts
    last = splits - 1
    me = lax.axis_index("base")
    own = lax.axis_index("exp")
    barrier = pltpu.get_barrier_semaphore()

    def load(j):
        slot = j % 2
        return (
            pltpu.make_async_copy(gate_ref.at[j], gate_buf.at[slot], load_sem.at[0, slot]),
            pltpu.make_async_copy(up_ref.at[j], up_buf.at[slot], load_sem.at[1, slot]),
        )

    def load_down(j):
        return pltpu.make_async_copy(down_ref.at[j], down_buf.at[j], down_sem.at[j])

    for j in range(min(2, experts)):
        for copy in load(j):
            copy.start()

    for off in range(1, splits):
        pl.semaphore_signal(
            barrier,
            inc=1,
            device_id={"base": lax.rem(me + off, splits)},
            device_id_type=pl.DeviceIdType.MESH,
        )
    for off in range(1, groups):
        pl.semaphore_signal(
            barrier,
            inc=1,
            device_id={"exp": lax.rem(own + off, groups)},
            device_id_type=pl.DeviceIdType.MESH,
        )
    pl.semaphore_wait(barrier, last + groups - 1)

    def base_copy(off, block):
        return pltpu.make_async_remote_copy(
            src_ref=base_ref,
            dst_ref=bases.at[block],
            send_sem=base_send.at[off],
            recv_sem=base_recv.at[block],
            device_id={"exp": lax.rem(own + off, groups)},
            device_id_type=pl.DeviceIdType.MESH,
        )

    for off in range(1, groups):
        base_copy(off, own).start()
    bases[own] = base_ref[...]

    def passing(item, source, way):
        step = 1 if way == 0 else -1
        ref = lows.at[source] if item == experts else hidden.at[source, item]
        return pltpu.make_async_remote_copy(
            src_ref=ref,
            dst_ref=ref,
            send_sem=send_sem.at[way, source, item],
            recv_sem=recv_sem.at[source, item],
            device_id={"base": me + step},
            device_id_type=pl.DeviceIdType.MESH,
        )

    def relay(item, far):
        if far == 0:
            for way, inside in ((0, me < last), (1, me > 0)):

                @pl.when(inside)
                def _(way=way):
                    passing(item, me, way).start()

            return
        for way, source, inside, on in (
            (0, me - far, me >= far, me < last),
            (1, me + far, me + far <= last, me > 0),
        ):

            @pl.when(inside)
            def _(way=way, source=source):
                passing(item, source, way).wait_recv()

            @pl.when(jnp.logical_and(inside, on))
            def _(way=way, source=source):
                passing(item, source, way).start()

    lows[me] = low_ref[...]
    relay(experts, 0)

    chunk = tile_of(depth, (1024, 512, 256, 128))
    tile = tile_of(local_width, (256, 128))

    def first_half(j):
        for copy in load(j):
            copy.wait()
        slot = j % 2
        gate_acc[...] = jnp.zeros_like(gate_acc)
        up_acc[...] = jnp.zeros_like(up_acc)

        @pl.loop(0, depth // chunk)
        def _(c):
            part = pl.ds(pl.multiple_of(c * chunk, chunk), chunk)
            block = rows_ref[:, part]
            gate_acc[...] += jnp.dot(
                block, gate_buf[slot, part, :], preferred_element_type=jnp.float32
            )
            up_acc[...] += jnp.dot(block, up_buf[slot, part, :], preferred_element_type=jnp.float32)

        if j + 2 < experts:
            for copy in load(j + 2):
                copy.start()
        load_down(j).start()
        value = gate_acc[...]
        both = (value / (1.0 + jnp.exp(-value)) * up_acc[...]).astype(jnp.bfloat16)
        hidden[me, j] = jnp.dot(
            select_ref[j], both, preferred_element_type=jnp.float32
        ).astype(jnp.bfloat16)

    def second_half(j):
        load_down(j).wait()
        picked = []
        for b in range(splits):
            chosen = jnp.dot(select_ref[j], lows[b], preferred_element_type=jnp.float32)
            picked.append(chosen[:, j * low_width : (j + 1) * low_width].astype(jnp.bfloat16))

        @pl.loop(0, local_width // tile)
        def _(c):
            part = pl.ds(pl.multiple_of(c * tile, tile), tile)
            total = jnp.zeros((out_ref.shape[1], tile), jnp.float32)
            for b in range(splits):
                total += jnp.dot(
                    hidden[b, j],
                    down_buf[j, b * width : (b + 1) * width, part],
                    preferred_element_type=jnp.float32,
                )
            for b in range(splits):
                total -= jnp.dot(
                    picked[b],
                    low_down_ref[j, b * low_width : (b + 1) * low_width, part],
                    preferred_element_type=jnp.float32,
                )
            out_ref[j, :, part] = total.astype(jnp.bfloat16)

    for step in range(experts + last):
        if step < experts:
            first_half(step)
            relay(step, 0)
        for far in range(1, splits):
            if far == step + 1:
                relay(experts, far)
            if 0 <= step - far < experts:
                relay(step - far, far)
        if step >= last:
            second_half(step - last)

    for off in range(1, groups):
        arrived = base_copy(off, lax.rem(own + off, groups))
        arrived.wait_recv()
        arrived.wait_send()

    for item in range(experts + 1):
        for source in range(splits):
            for way, inside in (
                (0, jnp.logical_and(me >= source, me < last)),
                (1, jnp.logical_and(me <= source, me > 0)),
            ):

                @pl.when(inside)
                def _(item=item, source=source, way=way):
                    passing(item, source, way).wait_send()


def run_experts(rows, select, low_all, gate, up, down, low_down, base_own, splits, groups):
    experts, depth, width = gate.shape
    slots = select.shape[1]
    all_rows = rows.shape[0]
    local_width = down.shape[2]
    vmem, hbm = pl.BlockSpec(memory_space=pltpu.VMEM), pl.BlockSpec(memory_space=pl.ANY)
    flops = 2 * experts * (2 * all_rows * depth * width + slots * splits * width * local_width)
    moved = 2 * experts * (2 * depth * width + splits * width * local_width)
    return pl.pallas_call(
        functools.partial(expert_kernel, splits, groups),
        out_shape=(
            jax.ShapeDtypeStruct((experts, slots, local_width), jnp.bfloat16),
            jax.ShapeDtypeStruct((groups,) + base_own.shape, jnp.bfloat16),
        ),
        in_specs=[vmem, vmem, vmem, hbm, hbm, hbm, vmem, vmem],
        out_specs=(vmem, vmem),
        scratch_shapes=[
            pltpu.VMEM((2, depth, width), jnp.bfloat16),
            pltpu.VMEM((2, depth, width), jnp.bfloat16),
            pltpu.VMEM(down.shape, jnp.bfloat16),
            pltpu.VMEM((splits, experts, slots, width), jnp.bfloat16),
            pltpu.VMEM((splits,) + low_all.shape, jnp.bfloat16),
            pltpu.VMEM((all_rows, width), jnp.float32),
            pltpu.VMEM((all_rows, width), jnp.float32),
            pltpu.SemaphoreType.DMA((2, 2)),
            pltpu.SemaphoreType.DMA((experts,)),
            pltpu.SemaphoreType.DMA((2, splits, experts + 1)),
            pltpu.SemaphoreType.DMA((splits, experts + 1)),
            pltpu.SemaphoreType.DMA((groups,)),
            pltpu.SemaphoreType.DMA((groups,)),
        ],
        compiler_params=pltpu.CompilerParams(
            collective_id=1, has_side_effects=True, vmem_limit_bytes=54 * 1024 * 1024
        ),
        cost_estimate=pl.CostEstimate(flops=flops, bytes_accessed=moved, transcendentals=0),
    )(rows, select, low_all, gate, up, down, low_down, base_own)


def swiglu(rows, gate_w, up_w):
    gate_pre = jnp.dot(rows, gate_w, preferred_element_type=jnp.float32)
    up_pre = jnp.dot(rows, up_w, preferred_element_type=jnp.float32)
    return (jax.nn.silu(gate_pre) * up_pre).astype(jnp.bfloat16)


def shards(
    tokens,
    expert_ids,
    gate_q,
    importance,
    dense_gate,
    dense_up,
    dense_down,
    delta_gate,
    delta_up,
    delta_down,
    base_gate,
    base_up,
    base_down,
):
    groups = lax.axis_size("exp")
    splits = lax.axis_size("base")
    tok_rows, local_width = tokens.shape
    top_k = expert_ids.shape[1]
    local_experts = dense_gate.shape[0]
    capacity = tok_rows * top_k * 3 // (2 * local_experts * groups)
    low_width = delta_gate.shape[2]
    all_rows = tok_rows * groups
    slots = capacity * groups

    routing = lax.all_gather(
        jnp.concatenate([expert_ids, gate_q], axis=1), "exp", axis=0, tiled=True
    )
    own_rows = lax.all_gather(tokens, "base", axis=1, tiled=True)
    rows = lax.all_gather(own_rows, "exp", axis=0, tiled=True)

    ids, gates = routing[:, :top_k], routing[:, top_k:]
    first = lax.axis_index("exp") * local_experts
    mine = first + jnp.arange(local_experts, dtype=jnp.int32)
    hit = ids[:, None, :] == mine[None, :, None]
    weight = jnp.sum(jnp.where(hit, gates[:, None, :].astype(jnp.float32), 0.0), axis=2) / 65536.0
    named = jnp.any(hit, axis=2)
    order = jnp.arange(all_rows, dtype=jnp.int32)
    block = order // tok_rows
    before = (block[:, None] == block[None, :]) & (order[None, :] < order[:, None])
    position = jnp.dot(
        before.astype(jnp.bfloat16), named.astype(jnp.bfloat16), preferred_element_type=jnp.float32
    ).astype(jnp.int32)
    slot = jnp.where(named, block[:, None] * capacity + position, -1)
    pick = jnp.arange(slots, dtype=jnp.int32)[None, :, None] == slot.T[:, None, :]
    select = pick.astype(jnp.bfloat16)

    shared = swiglu(own_rows, base_gate, base_up)
    partial_value = jnp.dot(shared, base_down, preferred_element_type=jnp.float32)
    base_own = lax.psum_scatter(
        partial_value.astype(jnp.bfloat16), "base", scatter_dimension=1, tiled=True
    )

    contract = (((1,), (1,)), ((), ()))
    low_gates = delta_gate.transpose(0, 2, 1).reshape(local_experts * low_width, -1)
    low_ups = delta_up.transpose(0, 2, 1).reshape(local_experts * low_width, -1)
    low_pre = lax.dot_general(rows, low_gates, contract, preferred_element_type=jnp.float32)
    low_up = lax.dot_general(rows, low_ups, contract, preferred_element_type=jnp.float32)
    low_all = (jax.nn.silu(low_pre) * low_up).astype(jnp.bfloat16)

    residuals, bases = run_experts(
        rows,
        select,
        low_all,
        dense_gate,
        dense_up,
        dense_down,
        delta_down,
        base_own,
        splits,
        groups,
    )
    base_all = bases.reshape(all_rows, local_width)

    total = jnp.zeros((all_rows,), jnp.float32)
    for j in range(local_experts):
        residual = residuals[j].astype(jnp.float32)
        base_rows = jnp.dot(select[j], base_all, preferred_element_type=jnp.float32)
        deviation = residual - base_rows
        squares = jnp.sum(importance * deviation * deviation, axis=1)
        back = jnp.sum(jnp.where(pick[j], squares[:, None], 0.0), axis=0)
        total = total + weight[:, j] * back
    return sum_over_group(total / D, groups, splits)


def solution(mesh):
    in_specs = (
        P(("grp", "exp"), "base"),
        P(("grp", "exp"), None),
        P(("grp", "exp"), None),
        P("base"),
        P("exp", None, "base"),
        P("exp", None, "base"),
        P("exp", None, "base"),
        P("exp", None, "base"),
        P("exp", None, "base"),
        P("exp", None, "base"),
        P(None, "base"),
        P(None, "base"),
        P("base", None),
    )
    out_specs = P(("grp", "exp"))
    return jax.shard_map(shards, mesh=mesh, in_specs=in_specs, out_specs=out_specs, check_vma=False)
```
